256 devices in a mesh: outer: 16 (over z, y_lo), dev: 16 (over x, y_hi, core).
Axes of the slice: x: 4, y: 4 (y_hi: 2, y_lo: 2; y = y_hi * 2 + y_lo), z: 8, core: 2. Of those that a mesh axis runs over, the one named last changes fastest.
Arguments:
- partials: bfloat16 [256, 8192, 256], P(('outer', 'dev')), may hold values from -6 to 6
- p_old: bfloat16 [8192, 1024], P('dev'), may hold values from -0.0625 to 0.0625
- p_new: bfloat16 [8192, 1024], P('dev'), may hold values from -0.0625 to 0.0625
- weight: float32 [8192, 256], P('dev'), may hold values from -4 to 4
- m_old: float32 [1024, 256], P('dev'), may hold values from -96 to 96
- v_old: float32 [1024, 256], P('dev'), may hold values from 32 to 1280
Outputs:
- new_weight: float32 [8192, 256], P('dev')
- m_new: float32 [1024, 256], P('dev')
- v_new: float32 [1024, 256], P('dev')
The draws below stay inside these ranges and needn't reach their ends.
All inputs are finite; a program needn't handle non-finite values.
Results may differ from the reference program's by a relative error of at most 0.0012.
Values may be sent and summed in bfloat16 or wider, within the bound.
No kernel may reach another device: no remote copies, remote signals or barrier semaphores. Data moves between devices by JAX's collectives and lax.ppermute only.
A program may use at most 128 MiB of HBM per device.

```python
import math
import jax
import jax.numpy as jnp
from jax import lax

D = 8192
R = 1024
COLS = 256
DEVICES = 256


def levels(own_key, extent, shards, smallest, top_value):
    gain, own = 1.0, jax.random.fold_in(own_key, 6)
    for axis_at, shards_of in shards:
        heights = jnp.exp(jax.random.uniform(jax.random.fold_in(own, axis_at), (shards_of,), jnp.float32, smallest / len(shards), top_value / len(shards)))
        gain = gain * jnp.repeat(heights, extent[axis_at] // shards_of).reshape([-1 if axis == axis_at else 1 for axis in range(len(extent))])
    return gain


def centred(own_key, dims, deviation, limit, split=(), held_as=jnp.bfloat16):
    values = deviation * jax.random.normal(own_key, dims, jnp.float32)
    if split:
        values = values * levels(own_key, dims, split, -0.22, 0.18)
    return jnp.clip(values, -limit, limit).astype(held_as)


def setup_inputs(seed: int = 0) -> dict:
    streams_of = jax.random.split(jax.random.key(seed), 7)
    return {
        "partials": centred(streams_of[0], (DEVICES, D, COLS), 1.0, 6.0, ((0, 256),)),
        "p_old": centred(streams_of[1], (D, R), D ** -0.5, 0.0625, ((0, 16),)),
        "p_new": centred(streams_of[2], (D, R), D ** -0.5, 0.0625, ((0, 16),)),
        "weight": centred(streams_of[3], (D, COLS), 0.3, 4.0, ((0, 16),), jnp.float32),
        "m_old": centred(streams_of[4], (R, COLS), 16.0, 96.0, ((0, 16),), jnp.float32),
        "v_old": jnp.clip(jnp.exp(math.log(1280.0) - 3.6888795 * jax.random.uniform(streams_of[5], (R, COLS), jnp.float32) ** levels(streams_of[5], (R, COLS), ((0, 16),), -0.2, 0.2)), 32.0, 1280.0),
    }


beta_mean = 0.9
beta_square = 0.95
bias_mean = 0.9999734386011124
bias_square = 0.9940794707796659
adam_epsilon = 1e-08
step_scale = 0.5

def reference(partials, p_old, p_new, weight, m_old, v_old):

    def accumulate(total, piece):
        return (total + piece.astype(jnp.float32), None)
    grad, _ = lax.scan(accumulate, jnp.zeros((D, COLS), jnp.float32), partials)
    projected = jnp.dot(p_new.astype(jnp.float32).T, grad, precision=lax.Precision.HIGHEST)
    margin = jnp.dot(p_new.T, p_old, preferred_element_type=jnp.float32)
    m_rot = jnp.dot(margin, m_old, precision=lax.Precision.HIGHEST)
    v_rot = jnp.dot(margin * margin, v_old, precision=lax.Precision.HIGHEST)
    m_new = beta_mean * m_rot + (1.0 - beta_mean) * projected
    v_new = beta_square * v_rot + (1.0 - beta_square) * projected * projected
    direction = (m_new / bias_mean / (jnp.sqrt(v_new / bias_square) + adam_epsilon)).astype(jnp.bfloat16)
    update = jnp.dot(p_new, direction, preferred_element_type=jnp.float32)
    new_weight = weight - step_scale * update
    return (new_weight, m_new, v_new)
```

```python
import jax
import jax.numpy as jnp
from jax import lax
from jax.sharding import Mesh, PartitionSpec as P

beta_mean = 0.9
beta_square = 0.95
bias_mean = 0.9999734386011124
bias_square = 0.9940794707796659
adam_epsilon = 1e-08
step_scale = 0.5

AXES = ("z", "yl", "x", "yh", "core")
SIZES = (8, 2, 4, 2, 2)
OUTER = ("z", "yl")
DEV = ("x", "yh", "core")
PLANE = ("x", "yh", "yl")
PAIRS = ("x", "yh")
SCALE = 4096.0


def swap(value, axis, bit, size):
    return lax.ppermute(value, axis, [(i, i ^ bit) for i in range(size)])


def cut(value, at, extent, axis):
    return lax.dynamic_slice_in_dim(value, at * extent, extent, axis)


def pieces(value):
    high = lax.reduce_precision(value, 8, 7)
    rest = value - high
    mid = lax.reduce_precision(rest, 8, 7)
    low = rest - mid
    return jnp.concatenate([high, mid, low], axis=1).astype(jnp.bfloat16)


def on_device(partials, p_old, p_new, weight, m_old, v_old):
    core = lax.axis_index("core")
    z, yl, yh, x = (lax.axis_index(name) for name in ("z", "yl", "yh", "x"))
    f32 = jnp.float32

    grad = partials[0]
    theirs = swap(cut(grad, 1 - core, 128, 1), "core", 1, 2)
    ours = cut(grad, core, 128, 1)
    chip_sum = ((ours.astype(f32) + theirs.astype(f32)) * SCALE).astype(jnp.float16)
    rows = lax.all_to_all(chip_sum.reshape(8, 1024, 128), PAIRS, 0, 0, tiled=True)

    p_other = swap(p_new, "core", 1, 2)

    moments = jnp.stack([m_old, v_old])
    moments_in = swap(cut(moments, 1 - core, 128, 2), "core", 1, 2)
    moments_own = cut(moments, core, 128, 2)
    moments = jnp.where(
        core == 0,
        jnp.concatenate([moments_own, moments_in], axis=1),
        jnp.concatenate([moments_in, moments_own], axis=1),
    )
    turn = [(a * 8 + b, b * 8 + a) for a in range(8) for b in range(8)]
    moments = lax.ppermute(moments, ("z", "x", "yh"), turn)

    p_rank = lax.dynamic_index_in_dim(p_new.reshape(512, 8, 2, 64), yl, 2, keepdims=False)
    margin = jnp.dot(
        p_rank.reshape(512, 512).T, cut(p_old, z, 128, 1), preferred_element_type=f32
    )
    margin = margin + swap(margin, "core", 1, 2)
    margin = margin.reshape(2, 2, 2, 64, 128)
    hi, lo = x // 2, x % 2

    def halve(value, place, axis, bit, size):
        keep = lax.dynamic_index_in_dim(value, place, 0, keepdims=False)
        give = lax.dynamic_index_in_dim(value, 1 - place, 0, keepdims=False)
        return keep + swap(give, axis, bit, size)

    margin = halve(margin, hi, "x", 2, 4)
    margin = halve(margin, lo, "x", 1, 4)
    margin = halve(margin, yh, "yh", 1, 2)
    first = jnp.dot(margin, moments[0], precision=lax.Precision.HIGHEST)
    second = jnp.dot(margin * margin, moments[1], precision=lax.Precision.HIGHEST)
    rotated = jnp.stack([first, second])
    for bit in (1, 2, 4):
        rotated = rotated + swap(rotated, "z", bit, 8)

    grad_rows = jnp.sum(rows.astype(f32), axis=0) * (1.0 / SCALE)
    split = pieces(grad_rows)
    across = (((0,), (0,)), ((), ()))
    terms = lax.dot_general(
        p_new, cut(split, core, 512, 0), across, preferred_element_type=f32
    ) + lax.dot_general(
        p_other, cut(split, 1 - core, 512, 0), across, preferred_element_type=f32
    )
    projected = terms[:, :128] + terms[:, 128:256] + terms[:, 256:]
    projected = lax.all_to_all(projected.reshape(16, 64, 128), PLANE, 0, 0, tiled=True)
    projected = jnp.sum(projected, axis=0)
    for bit in (1, 2, 4):
        projected = projected + swap(projected, "z", bit, 8)

    m_new = beta_mean * rotated[0] + (1.0 - beta_mean) * projected
    v_new = beta_square * rotated[1] + (1.0 - beta_square) * projected * projected
    direction = (m_new / bias_mean / (jnp.sqrt(v_new / bias_square) + adam_epsilon)).astype(
        jnp.bfloat16
    )

    def sides(own, other, axis):
        return jnp.where(
            core == 0,
            jnp.concatenate([own, other], axis=axis),
            jnp.concatenate([other, own], axis=axis),
        )

    spread = jnp.broadcast_to(direction[None], (16, 64, 128))
    mine = lax.all_to_all(spread, PLANE, 0, 0, tiled=True).reshape(1024, 128)
    other = swap(mine, "core", 1, 2)
    update = sides(
        jnp.dot(p_new, mine, preferred_element_type=f32),
        jnp.dot(p_new, other, preferred_element_type=f32),
        1,
    )
    new_weight = weight - step_scale * update

    made = jnp.stack([m_new, v_new])
    made = sides(made, swap(made, "core", 1, 2), 2)
    made = jnp.where(core == yl, made, swap(made, "yl", 1, 2))
    return (new_weight, made[0], made[1])


def solution(mesh):
    fine = Mesh(mesh.devices.reshape(SIZES), AXES)
    in_specs = (
        P(OUTER + DEV, None, None),
        P(DEV, None),
        P(DEV, None),
        P(DEV, None),
        P(DEV, None),
        P(DEV, None),
    )
    out_specs = (P(DEV, None), P(DEV, None), P(DEV, None))
    return jax.shard_map(
        on_device, mesh=fine, in_specs=in_specs, out_specs=out_specs, check_vma=False
    )
```

```python
import jax
import jax.numpy as jnp
from jax import lax
from jax.sharding import Mesh, PartitionSpec as P

beta_mean = 0.9
beta_square = 0.95
bias_mean = 0.9999734386011124
bias_square = 0.9940794707796659
adam_epsilon = 1e-08
step_scale = 0.5

AXES = ("z", "yl", "x", "yh", "core")
SIZES = (8, 2, 4, 2, 2)
OUTER = ("z", "yl")
DEV = ("x", "yh", "core")
PLANE = ("x", "yh", "yl")
PAIRS = ("x", "yh")
SCALE = 4096.0
MARGIN_SCALE = 8192.0
PROJECTED_SCALE = 8.0


def swap(value, axis, bit, size):
    return lax.ppermute(value, axis, [(i, i ^ bit) for i in range(size)])


def cut(value, at, extent, axis):
    return lax.dynamic_slice_in_dim(value, at * extent, extent, axis)


def pieces(value):
    high = lax.reduce_precision(value, 8, 7)
    rest = value - high
    mid = lax.reduce_precision(rest, 8, 7)
    low = rest - mid
    return jnp.concatenate([high, mid, low], axis=1).astype(jnp.bfloat16)


def on_device(partials, p_old, p_new, weight, m_old, v_old):
    core = lax.axis_index("core")
    z, yl = lax.axis_index("z"), lax.axis_index("yl")
    f32 = jnp.float32

    def sides(own, other, axis):
        return jnp.where(
            core == 0,
            jnp.concatenate([own, other], axis=axis),
            jnp.concatenate([other, own], axis=axis),
        )

    p_other = swap(p_new, "core", 1, 2)

    turn = [(a * 8 + b, a * 8 + (a ^ b)) for a in range(8) for b in range(8)]
    turned = lax.ppermute(jnp.stack([m_old, v_old]), ("z", "x", "yh"), turn)

    p_rank = lax.dynamic_index_in_dim(p_new.reshape(512, 8, 2, 64), yl, 2, keepdims=False)
    product = jnp.dot(p_rank.reshape(512, 512).T, p_old, preferred_element_type=f32)
    met = (lax.broadcasted_iota(jnp.int32, (512, 128), 0) // 64) ^ z
    margin = product[:, :128]
    for place in range(1, 8):
        margin = jnp.where(met == place, product[:, place * 128 : place * 128 + 128], margin)
    margin = margin + swap(margin, "core", 1, 2)
    margin = (margin * MARGIN_SCALE).astype(jnp.float16).reshape(8, 64, 128)

    grad = partials[0]
    theirs = swap(cut(grad, 1 - core, 128, 1), "core", 1, 2)
    ours = cut(grad, core, 128, 1)
    chip_sum = ((ours.astype(f32) + theirs.astype(f32)) * SCALE).astype(jnp.float16)
    sent = jnp.concatenate([chip_sum.reshape(8, 1024, 128), margin], axis=1)
    sent, turned = lax.optimization_barrier((sent, turned))
    rows = lax.all_to_all(sent, PAIRS, 0, 0, tiled=True)

    moments_in = swap(cut(turned, 1 - core, 128, 2), "core", 1, 2)
    moments = sides(cut(turned, core, 128, 2), moments_in, 1)
    margin = jnp.sum(rows[:, 1024:].astype(f32), axis=0) * (1.0 / MARGIN_SCALE)
    first = jnp.dot(margin, moments[0], precision=lax.Precision.HIGHEST)
    second = jnp.dot(margin * margin, moments[1], precision=lax.Precision.HIGHEST)
    rotated = jnp.stack([first, second])
    for bit in (1, 2, 4):
        rotated = rotated + swap(rotated, "z", bit, 8)

    grad_rows = jnp.sum(rows[:, :1024].astype(f32), axis=0) * (1.0 / SCALE)
    split = pieces(grad_rows)
    across = (((0,), (0,)), ((), ()))
    terms = lax.dot_general(
        p_new, cut(split, core, 512, 0), across, preferred_element_type=f32
    ) + lax.dot_general(
        p_other, cut(split, 1 - core, 512, 0), across, preferred_element_type=f32
    )
    projected = terms[:, :128] + terms[:, 128:256] + terms[:, 256:]
    projected = (projected * PROJECTED_SCALE).astype(jnp.float16)
    projected = lax.all_to_all(projected.reshape(16, 64, 128), PLANE, 0, 0, tiled=True)
    projected = jnp.sum(projected.astype(f32), axis=0) * (1.0 / PROJECTED_SCALE)
    for bit in (1, 2, 4):
        projected = projected + swap(projected, "z", bit, 8)

    m_new = beta_mean * rotated[0] + (1.0 - beta_mean) * projected
    v_new = beta_square * rotated[1] + (1.0 - beta_square) * projected * projected
    direction = (m_new / bias_mean / (jnp.sqrt(v_new / bias_square) + adam_epsilon)).astype(
        jnp.bfloat16
    )

    spread = jnp.broadcast_to(direction[None], (16, 64, 128))
    mine = lax.all_to_all(spread, PLANE, 0, 0, tiled=True).reshape(1024, 128)
    other = swap(mine, "core", 1, 2)
    update = sides(
        jnp.dot(p_new, mine, preferred_element_type=f32),
        jnp.dot(p_new, other, preferred_element_type=f32),
        1,
    )
    new_weight = weight - step_scale * update

    made = jnp.stack([m_new, v_new])
    near = swap(made, "yl", 1, 2)
    kept = jnp.where(core == yl, made, near)
    given = jnp.where(core == yl, near, made)
    made = sides(kept, swap(given, "core", 1, 2), 2)
    return (new_weight, made[0], made[1])


def solution(mesh):
    fine = Mesh(mesh.devices.reshape(SIZES), AXES)
    in_specs = (
        P(OUTER + DEV, None, None),
        P(DEV, None),
        P(DEV, None),
        P(DEV, None),
        P(DEV, None),
        P(DEV, None),
    )
    out_specs = (P(DEV, None), P(DEV, None), P(DEV, None))
    return jax.shard_map(
        on_device, mesh=fine, in_specs=in_specs, out_specs=out_specs, check_vma=False
    )
```

```python
import jax
import jax.numpy as jnp
from jax import lax
from jax.sharding import Mesh, PartitionSpec as P

beta_mean = 0.9
beta_square = 0.95
bias_mean = 0.9999734386011124
bias_square = 0.9940794707796659
adam_epsilon = 1e-08
step_scale = 0.5

AXES = ("z", "yl", "x", "yh", "core")
SIZES = (8, 2, 4, 2, 2)
OUTER = ("z", "yl")
DEV = ("x", "yh", "core")
PLANE = ("x", "yh", "yl")
PAIRS = ("x", "yh")
SCALE = 4096.0
MARGIN_SCALE = 8192.0
PROJECTED_SCALE = 8.0


def swap(value, axis, bit, size):
    return lax.ppermute(value, axis, [(i, i ^ bit) for i in range(size)])


def cut(value, at, extent, axis):
    return lax.dynamic_slice_in_dim(value, at * extent, extent, axis)


def pieces(value):
    high = lax.reduce_precision(value, 8, 7)
    rest = value - high
    return jnp.concatenate([high, rest], axis=1).astype(jnp.bfloat16)


def on_device(partials, p_old, p_new, weight, m_old, v_old):
    core = lax.axis_index("core")
    z, yl = lax.axis_index("z"), lax.axis_index("yl")
    f32 = jnp.float32

    def sides(own, other, axis):
        return jnp.where(
            core == 0,
            jnp.concatenate([own, other], axis=axis),
            jnp.concatenate([other, own], axis=axis),
        )

    p_other = swap(p_new, "core", 1, 2)

    turn = [(a * 8 + b, a * 8 + (a ^ b)) for a in range(8) for b in range(8)]
    moments = jnp.stack([m_old, v_old])
    moments_in = swap(cut(moments, 1 - core, 128, 2), "core", 1, 2)
    moments = sides(cut(moments, core, 128, 2), moments_in, 1)
    moments = lax.ppermute(moments, ("z", "x", "yh"), turn)

    p_rank = lax.dynamic_index_in_dim(p_new.reshape(512, 8, 2, 64), yl, 2, keepdims=False)
    product = jnp.dot(p_rank.reshape(512, 512).T, p_old, preferred_element_type=f32)
    met = (lax.broadcasted_iota(jnp.int32, (512, 128), 0) // 64) ^ z
    margin = product[:, :128]
    for place in range(1, 8):
        margin = jnp.where(met == place, product[:, place * 128 : place * 128 + 128], margin)
    margin = margin + swap(margin, "core", 1, 2)
    margin = (margin * MARGIN_SCALE).astype(jnp.float16).reshape(8, 64, 128)

    grad = partials[0]
    theirs = swap(cut(grad, 1 - core, 128, 1), "core", 1, 2)
    ours = cut(grad, core, 128, 1)
    chip_sum = ((ours.astype(f32) + theirs.astype(f32)) * SCALE).astype(jnp.float16)
    sent = jnp.concatenate([chip_sum.reshape(8, 1024, 128), margin], axis=1)
    rows = lax.all_to_all(sent, PAIRS, 0, 0, tiled=True)

    grad_rows = jnp.sum(rows[:, :1024].astype(f32), axis=0) * (1.0 / SCALE)
    split = pieces(grad_rows)
    across = (((0,), (0,)), ((), ()))
    terms = lax.dot_general(
        p_new, cut(split, core, 512, 0), across, preferred_element_type=f32
    ) + lax.dot_general(
        p_other, cut(split, 1 - core, 512, 0), across, preferred_element_type=f32
    )
    projected = terms[:, :128] + terms[:, 128:]
    projected = (projected * PROJECTED_SCALE).astype(jnp.float16)
    projected, rows = lax.optimization_barrier((projected, rows))
    projected = lax.all_to_all(projected.reshape(16, 64, 128), PLANE, 0, 0, tiled=True)
    projected = jnp.sum(projected.astype(f32), axis=0) * (1.0 / PROJECTED_SCALE)
    margin = jnp.sum(rows[:, 1024:].astype(f32), axis=0) * (1.0 / MARGIN_SCALE)
    first = jnp.dot(margin, moments[0], precision=lax.Precision.HIGHEST)
    second = jnp.dot(margin * margin, moments[1], precision=lax.Precision.HIGHEST)
    shares = jnp.stack([projected, first, second])
    for bit in (1, 2, 4):
        shares = shares + swap(shares, "z", bit, 8)
    projected, first, second = shares[0], shares[1], shares[2]

    m_new = beta_mean * first + (1.0 - beta_mean) * projected
    v_new = beta_square * second + (1.0 - beta_square) * projected * projected
    direction = (m_new / bias_mean / (jnp.sqrt(v_new / bias_square) + adam_epsilon)).astype(
        jnp.bfloat16
    )

    spread = jnp.broadcast_to(direction[None], (16, 64, 128))
    mine = lax.all_to_all(spread, PLANE, 0, 0, tiled=True).reshape(1024, 128)
    made = jnp.stack([m_new, v_new])
    near = swap(made, "yl", 1, 2)
    near, mine = lax.optimization_barrier((near, mine))
    other = swap(mine, "core", 1, 2)
    update = sides(
        jnp.dot(p_new, mine, preferred_element_type=f32),
        jnp.dot(p_new, other, preferred_element_type=f32),
        1,
    )
    new_weight = weight - step_scale * update

    kept = jnp.where(core == yl, made, near)
    given = jnp.where(core == yl, near, made)
    made = sides(kept, swap(given, "core", 1, 2), 2)
    return (new_weight, made[0], made[1])


def solution(mesh):
    fine = Mesh(mesh.devices.reshape(SIZES), AXES)
    in_specs = (
        P(OUTER + DEV, None, None),
        P(DEV, None),
        P(DEV, None),
        P(DEV, None),
        P(DEV, None),
        P(DEV, None),
    )
    out_specs = (P(DEV, None), P(DEV, None), P(DEV, None))
    return jax.shard_map(
        on_device, mesh=fine, in_specs=in_specs, out_specs=out_specs, check_vma=False
    )
```

```python
import jax
import jax.numpy as jnp
from jax import lax
from jax.sharding import Mesh, PartitionSpec as P

beta_mean = 0.9
beta_square = 0.95
bias_mean = 0.9999734386011124
bias_square = 0.9940794707796659
adam_epsilon = 1e-08
step_scale = 0.5

AXES = ("z", "yl", "x", "yh", "core")
SIZES = (8, 2, 4, 2, 2)
OUTER = ("z", "yl")
DEV = ("x", "yh", "core")
PLANE = ("x", "yh", "yl")
PAIRS = ("x", "yh")
SCALE = 4096.0
MARGIN_SCALE = 8192.0
PROJECTED_SCALE = 8.0


def swap(value, axis, bit, size):
    return lax.ppermute(value, axis, [(i, i ^ bit) for i in range(size)])


def cut(value, at, extent, axis):
    return lax.dynamic_slice_in_dim(value, at * extent, extent, axis)


def pieces(value):
    high = lax.reduce_precision(value, 8, 7)
    rest = value - high
    return jnp.concatenate([high, rest], axis=1).astype(jnp.bfloat16)


def on_device(partials, p_old, p_new, weight, m_old, v_old):
    core = lax.axis_index("core")
    z, yl = lax.axis_index("z"), lax.axis_index("yl")
    f32 = jnp.float32

    def sides(own, other, axis):
        return jnp.where(
            core == 0,
            jnp.concatenate([own, other], axis=axis),
            jnp.concatenate([other, own], axis=axis),
        )

    p_other = swap(p_new, "core", 1, 2)

    turn = [(a * 8 + b, a * 8 + (a ^ b)) for a in range(8) for b in range(8)]
    turned = lax.ppermute(jnp.stack([m_old, v_old]), ("z", "x", "yh"), turn)

    p_rank = lax.dynamic_index_in_dim(p_new.reshape(512, 8, 2, 64), yl, 2, keepdims=False)
    product = jnp.dot(p_rank.reshape(512, 512).T, p_old, preferred_element_type=f32)
    met = (lax.broadcasted_iota(jnp.int32, (512, 128), 0) // 64) ^ z
    margin = product[:, :128]
    for place in range(1, 8):
        margin = jnp.where(met == place, product[:, place * 128 : place * 128 + 128], margin)
    margin = margin + swap(margin, "core", 1, 2)
    margin = (margin * MARGIN_SCALE).astype(jnp.float16).reshape(8, 64, 128)

    grad = partials[0]
    theirs = cut(swap(grad, "core", 1, 2), core, 128, 1)
    ours = cut(grad, core, 128, 1)
    chip_sum = ((ours.astype(f32) + theirs.astype(f32)) * SCALE).astype(jnp.float16)
    sent = jnp.concatenate([chip_sum.reshape(8, 1024, 128), margin], axis=1)
    sent, turned = lax.optimization_barrier((sent, turned))
    rows = lax.all_to_all(sent, PAIRS, 0, 0, tiled=True)

    grad_rows = jnp.sum(rows[:, :1024].astype(f32), axis=0) * (1.0 / SCALE)
    split = pieces(grad_rows)
    across = (((0,), (0,)), ((), ()))
    terms = lax.dot_general(
        p_new, cut(split, core, 512, 0), across, preferred_element_type=f32
    ) + lax.dot_general(
        p_other, cut(split, 1 - core, 512, 0), across, preferred_element_type=f32
    )
    projected = terms[:, :128] + terms[:, 128:]
    projected = (projected * PROJECTED_SCALE).astype(jnp.float16)
    projected, rows = lax.optimization_barrier((projected, rows))
    projected = lax.all_to_all(projected.reshape(16, 64, 128), PLANE, 0, 0, tiled=True)
    projected = jnp.sum(projected.astype(f32), axis=0) * (1.0 / PROJECTED_SCALE)
    moments_in = swap(cut(turned, 1 - core, 128, 2), "core", 1, 2)
    moments = sides(cut(turned, core, 128, 2), moments_in, 1)
    margin = jnp.sum(rows[:, 1024:].astype(f32), axis=0) * (1.0 / MARGIN_SCALE)
    first = jnp.dot(margin, moments[0], precision=lax.Precision.HIGHEST)
    second = jnp.dot(margin * margin, moments[1], precision=lax.Precision.HIGHEST)
    shares = jnp.stack([projected, first, second])
    for bit in (1, 2, 4):
        shares = shares + swap(shares, "z", bit, 8)
    projected, first, second = shares[0], shares[1], shares[2]

    m_new = beta_mean * first + (1.0 - beta_mean) * projected
    v_new = beta_square * second + (1.0 - beta_square) * projected * projected
    direction = (m_new / bias_mean / (jnp.sqrt(v_new / bias_square) + adam_epsilon)).astype(
        jnp.bfloat16
    )

    spread = jnp.broadcast_to(direction[None], (16, 64, 128))
    mine = lax.all_to_all(spread, PLANE, 0, 0, tiled=True).reshape(1024, 128)
    made = jnp.stack([m_new, v_new])
    near = swap(made, "yl", 1, 2)
    near, mine = lax.optimization_barrier((near, mine))
    other = swap(mine, "core", 1, 2)
    update = sides(
        jnp.dot(p_new, mine, preferred_element_type=f32),
        jnp.dot(p_new, other, preferred_element_type=f32),
        1,
    )
    new_weight = weight - step_scale * update

    kept = jnp.where(core == yl, made, near)
    given = jnp.where(core == yl, near, made)
    made = sides(kept, swap(given, "core", 1, 2), 2)
    return (new_weight, made[0], made[1])


def solution(mesh):
    fine = Mesh(mesh.devices.reshape(SIZES), AXES)
    in_specs = (
        P(OUTER + DEV, None, None),
        P(DEV, None),
        P(DEV, None),
        P(DEV, None),
        P(DEV, None),
        P(DEV, None),
    )
    out_specs = (P(DEV, None), P(DEV, None), P(DEV, None))
    return jax.shard_map(
        on_device, mesh=fine, in_specs=in_specs, out_specs=out_specs, check_vma=False
    )
```

```python
import jax
import jax.numpy as jnp
from jax import lax
from jax.sharding import Mesh, PartitionSpec as P

beta_mean = 0.9
beta_square = 0.95
bias_mean = 0.9999734386011124
bias_square = 0.9940794707796659
adam_epsilon = 1e-08
step_scale = 0.5

AXES = ("z", "yl", "x", "yh", "core")
SIZES = (8, 2, 4, 2, 2)
OUTER = ("z", "yl")
DEV = ("x", "yh", "core")
PLANE = ("x", "yh", "yl")
PAIRS = ("x", "yh")
SCALE = 4096.0
MARGIN_SCALE = 8192.0
PROJECTED_SCALE = 8.0
SHARE_SCALE = 2.0**-4
FIRST_SCALE = 2.0**-6
SECOND_SCALE = 2.0**-15
LOW_SCALE = 2.0**11


def swap(value, axis, bit, size):
    return lax.ppermute(value, axis, [(i, i ^ bit) for i in range(size)])


def cut(value, at, extent, axis):
    return lax.dynamic_slice_in_dim(value, at * extent, extent, axis)


def pieces(value):
    high = lax.reduce_precision(value, 8, 7)
    rest = value - high
    return jnp.concatenate([high, rest], axis=1).astype(jnp.bfloat16)


def packed_shares(projected, first, second):
    high = (first * FIRST_SCALE).astype(jnp.float16)
    high = lax.optimization_barrier(high)
    low = (first * FIRST_SCALE - high.astype(jnp.float32)) * LOW_SCALE
    rest = jnp.stack([low, projected * SHARE_SCALE, second * SECOND_SCALE])
    return jnp.concatenate([high[None], rest.astype(jnp.float16)])


def unpacked_shares(total):
    first = (total[0] + total[1] * (1.0 / LOW_SCALE)) * (1.0 / FIRST_SCALE)
    return total[2] * (1.0 / SHARE_SCALE), first, total[3] * (1.0 / SECOND_SCALE)


def on_device(partials, p_old, p_new, weight, m_old, v_old):
    core = lax.axis_index("core")
    z, yl = lax.axis_index("z"), lax.axis_index("yl")
    f32 = jnp.float32

    def sides(own, other, axis):
        return jnp.where(
            core == 0,
            jnp.concatenate([own, other], axis=axis),
            jnp.concatenate([other, own], axis=axis),
        )

    p_other = swap(p_new, "core", 1, 2)

    turn = [(a * 8 + b, a * 8 + (a ^ b)) for a in range(8) for b in range(8)]
    turned = lax.ppermute(jnp.stack([m_old, v_old]), ("z", "x", "yh"), turn)

    p_rank = lax.dynamic_index_in_dim(p_new.reshape(512, 8, 2, 64), yl, 2, keepdims=False)
    product = jnp.dot(p_rank.reshape(512, 512).T, p_old, preferred_element_type=f32)
    met = (lax.broadcasted_iota(jnp.int32, (512, 128), 0) // 64) ^ z
    margin = product[:, :128]
    for place in range(1, 8):
        margin = jnp.where(met == place, product[:, place * 128 : place * 128 + 128], margin)
    margin = margin + swap(margin, "core", 1, 2)
    margin = (margin * MARGIN_SCALE).astype(jnp.float16).reshape(8, 64, 128)

    grad = partials[0]
    theirs = cut(swap(grad, "core", 1, 2), core, 128, 1)
    ours = cut(grad, core, 128, 1)
    chip_sum = ((ours.astype(f32) + theirs.astype(f32)) * SCALE).astype(jnp.float16)
    sent = jnp.concatenate([chip_sum.reshape(8, 1024, 128), margin], axis=1)
    sent, turned = lax.optimization_barrier((sent, turned))
    rows = lax.all_to_all(sent, PAIRS, 0, 0, tiled=True)

    grad_rows = jnp.sum(rows[:, :1024].astype(f32), axis=0) * (1.0 / SCALE)
    split = pieces(grad_rows)
    across = (((0,), (0,)), ((), ()))
    terms = lax.dot_general(
        p_new, cut(split, core, 512, 0), across, preferred_element_type=f32
    ) + lax.dot_general(
        p_other, cut(split, 1 - core, 512, 0), across, preferred_element_type=f32
    )
    projected = terms[:, :128] + terms[:, 128:]
    projected = (projected * PROJECTED_SCALE).astype(jnp.float16)
    projected, rows = lax.optimization_barrier((projected, rows))
    projected = lax.all_to_all(projected.reshape(16, 64, 128), PLANE, 0, 0, tiled=True)
    projected = jnp.sum(projected.astype(f32), axis=0) * (1.0 / PROJECTED_SCALE)
    moments_in = swap(cut(turned, 1 - core, 128, 2), "core", 1, 2)
    moments = sides(cut(turned, core, 128, 2), moments_in, 1)
    margin = jnp.sum(rows[:, 1024:].astype(f32), axis=0) * (1.0 / MARGIN_SCALE)
    first = jnp.dot(margin, moments[0], precision=lax.Precision.HIGHEST)
    second = jnp.dot(margin * margin, moments[1], precision=lax.Precision.HIGHEST)
    shares = (projected, first, second)
    for bit in (1, 2, 4):
        packed = lax.optimization_barrier(packed_shares(*shares))
        ours, theirs = packed.astype(f32), swap(packed, "z", bit, 8).astype(f32)
        shares = unpacked_shares(ours + theirs)
    projected, first, second = shares

    m_new = beta_mean * first + (1.0 - beta_mean) * projected
    v_new = beta_square * second + (1.0 - beta_square) * projected * projected
    direction = (m_new / bias_mean / (jnp.sqrt(v_new / bias_square) + adam_epsilon)).astype(
        jnp.bfloat16
    )

    spread = jnp.broadcast_to(direction[None], (16, 64, 128))
    mine = lax.all_to_all(spread, PLANE, 0, 0, tiled=True).reshape(1024, 128)
    made = jnp.stack([m_new, v_new])
    near = swap(made, "yl", 1, 2)
    near, mine = lax.optimization_barrier((near, mine))
    other = swap(mine, "core", 1, 2)
    update = sides(
        jnp.dot(p_new, mine, preferred_element_type=f32),
        jnp.dot(p_new, other, preferred_element_type=f32),
        1,
    )
    new_weight = weight - step_scale * update

    kept = jnp.where(core == yl, made, near)
    given = jnp.where(core == yl, near, made)
    made = sides(kept, swap(given, "core", 1, 2), 2)
    return (new_weight, made[0], made[1])


def solution(mesh):
    fine = Mesh(mesh.devices.reshape(SIZES), AXES)
    in_specs = (
        P(OUTER + DEV, None, None),
        P(DEV, None),
        P(DEV, None),
        P(DEV, None),
        P(DEV, None),
        P(DEV, None),
    )
    out_specs = (P(DEV, None), P(DEV, None), P(DEV, None))
    return jax.shard_map(
        on_device, mesh=fine, in_specs=in_specs, out_specs=out_specs, check_vma=False
    )
```

```python
import jax
import jax.numpy as jnp
from jax import lax
from jax.sharding import Mesh, PartitionSpec as P

beta_mean = 0.9
beta_square = 0.95
bias_mean = 0.9999734386011124
bias_square = 0.9940794707796659
adam_epsilon = 1e-08
step_scale = 0.5

AXES = ("z", "yl", "x", "yh", "core")
SIZES = (8, 2, 4, 2, 2)
OUTER = ("z", "yl")
DEV = ("x", "yh", "core")
PLANE = ("x", "yh", "yl")
PAIRS = ("x", "yh")
SCALE = 4096.0
MARGIN_SCALE = 8192.0
PROJECTED_SCALE = 8.0
SHARE_SCALE = 2.0**-4
FIRST_SCALE = 2.0**-6
SECOND_SCALE = 2.0**-15
LOW_SCALE = 2.0**11


def swap(value, axis, bit, size):
    return lax.ppermute(value, axis, [(i, i ^ bit) for i in range(size)])


def cut(value, at, extent, axis):
    return lax.dynamic_slice_in_dim(value, at * extent, extent, axis)


def pieces(value):
    high = lax.reduce_precision(value, 8, 7)
    rest = value - high
    return jnp.concatenate([high, rest], axis=1).astype(jnp.bfloat16)


def packed_shares(projected, first, second):
    high = (first * FIRST_SCALE).astype(jnp.float16)
    high = lax.optimization_barrier(high)
    low = (first * FIRST_SCALE - high.astype(jnp.float32)) * LOW_SCALE
    rest = jnp.stack([low, projected * SHARE_SCALE, second * SECOND_SCALE])
    return jnp.concatenate([high[None], rest.astype(jnp.float16)])


def unpacked_shares(total):
    first = (total[0] + total[1] * (1.0 / LOW_SCALE)) * (1.0 / FIRST_SCALE)
    return total[2] * (1.0 / SHARE_SCALE), first, total[3] * (1.0 / SECOND_SCALE)


def on_device(partials, p_old, p_new, weight, m_old, v_old):
    core = lax.axis_index("core")
    z, yl = lax.axis_index("z"), lax.axis_index("yl")
    f32 = jnp.float32

    def sides(own, other, axis):
        return jnp.where(
            core == 0,
            jnp.concatenate([own, other], axis=axis),
            jnp.concatenate([other, own], axis=axis),
        )

    p_other = swap(p_new, "core", 1, 2)

    turn = [(a * 8 + b, a * 8 + (a ^ b)) for a in range(8) for b in range(8)]
    turned = lax.ppermute(jnp.stack([m_old, v_old]), ("z", "x", "yh"), turn)

    p_rank = lax.dynamic_index_in_dim(p_new.reshape(512, 8, 2, 64), yl, 2, keepdims=False)
    product = jnp.dot(p_rank.reshape(512, 512).T, p_old, preferred_element_type=f32)
    met = (lax.broadcasted_iota(jnp.int32, (512, 128), 0) // 64) ^ z
    margin = product[:, :128]
    for place in range(1, 8):
        margin = jnp.where(met == place, product[:, place * 128 : place * 128 + 128], margin)
    margin = margin + swap(margin, "core", 1, 2)
    margin = (margin * MARGIN_SCALE).astype(jnp.float16).reshape(8, 64, 128)

    grad = partials[0]
    theirs = cut(swap(grad, "core", 1, 2), core, 128, 1)
    ours = cut(grad, core, 128, 1)
    chip_sum = ((ours.astype(f32) + theirs.astype(f32)) * SCALE).astype(jnp.float16)
    sent = jnp.concatenate([chip_sum.reshape(8, 1024, 128), margin], axis=1)
    sent, turned = lax.optimization_barrier((sent, turned))
    rows = lax.all_to_all(sent, PAIRS, 0, 0, tiled=True)

    sums = lax.optimization_barrier(jnp.sum(rows.astype(f32), axis=0))
    grad_rows = sums[:1024] * (1.0 / SCALE)
    split = pieces(grad_rows)
    across = (((0,), (0,)), ((), ()))
    terms = lax.dot_general(
        p_new, cut(split, core, 512, 0), across, preferred_element_type=f32
    ) + lax.dot_general(
        p_other, cut(split, 1 - core, 512, 0), across, preferred_element_type=f32
    )
    projected = terms[:, :128] + terms[:, 128:]
    projected = (projected * PROJECTED_SCALE).astype(jnp.float16)
    projected, sums = lax.optimization_barrier((projected, sums))
    projected = lax.all_to_all(projected.reshape(16, 64, 128), PLANE, 0, 0, tiled=True)
    projected = jnp.sum(projected.astype(f32), axis=0) * (1.0 / PROJECTED_SCALE)
    moments_in = swap(cut(turned, 1 - core, 128, 2), "core", 1, 2)
    moments = sides(cut(turned, core, 128, 2), moments_in, 1)
    margin = sums[1024:] * (1.0 / MARGIN_SCALE)
    first = jnp.dot(margin, moments[0], precision=lax.Precision.HIGHEST)
    second = jnp.dot(margin * margin, moments[1], precision=lax.Precision.HIGHEST)
    shares = (projected, first, second)
    for bit in (1, 2, 4):
        packed = lax.optimization_barrier(packed_shares(*shares))
        ours, theirs = packed.astype(f32), swap(packed, "z", bit, 8).astype(f32)
        shares = unpacked_shares(ours + theirs)
    projected, first, second = shares

    m_new = beta_mean * first + (1.0 - beta_mean) * projected
    v_new = beta_square * second + (1.0 - beta_square) * projected * projected
    direction = (m_new / bias_mean / (jnp.sqrt(v_new / bias_square) + adam_epsilon)).astype(
        jnp.bfloat16
    )

    spread = jnp.broadcast_to(direction[None], (16, 64, 128))
    mine = lax.all_to_all(spread, PLANE, 0, 0, tiled=True).reshape(1024, 128)
    made = jnp.stack([m_new, v_new])
    near = swap(made, "yl", 1, 2)
    near, mine = lax.optimization_barrier((near, mine))
    other = swap(mine, "core", 1, 2)
    update = jnp.dot(p_new, sides(mine, other, 1), preferred_element_type=f32)
    new_weight = weight - step_scale * update

    kept = jnp.where(core == yl, made, near)
    given = jnp.where(core == yl, near, made)
    made = sides(kept, swap(given, "core", 1, 2), 2)
    return (new_weight, made[0], made[1])


def solution(mesh):
    fine = Mesh(mesh.devices.reshape(SIZES), AXES)
    in_specs = (
        P(OUTER + DEV, None, None),
        P(DEV, None),
        P(DEV, None),
        P(DEV, None),
        P(DEV, None),
        P(DEV, None),
    )
    out_specs = (P(DEV, None), P(DEV, None), P(DEV, None))
    return jax.shard_map(
        on_device, mesh=fine, in_specs=in_specs, out_specs=out_specs, check_vma=False
    )
```

```python
import jax
import jax.numpy as jnp
from jax import lax
from jax.experimental.layout import Layout, with_layout_constraint
from jax.sharding import Mesh, PartitionSpec as P

beta_mean = 0.9
beta_square = 0.95
bias_mean = 0.9999734386011124
bias_square = 0.9940794707796659
adam_epsilon = 1e-08
step_scale = 0.5

AXES = ("z", "yl", "x", "yh", "core")
SIZES = (8, 2, 4, 2, 2)
OUTER = ("z", "yl")
DEV = ("x", "yh", "core")
PLANE = ("x", "yh", "yl")
PAIRS = ("x", "yh")
SCALE = 4096.0
MARGIN_SCALE = 8192.0
PROJECTED_SCALE = 8.0
SHARE_SCALE = 2.0**-4
FIRST_SCALE = 2.0**-6
SECOND_SCALE = 2.0**-15
LOW_SCALE = 2.0**11


def swap(value, axis, bit, size):
    return lax.ppermute(value, axis, [(i, i ^ bit) for i in range(size)])


def cut(value, at, extent, axis):
    return lax.dynamic_slice_in_dim(value, at * extent, extent, axis)


def pieces(value):
    high = lax.reduce_precision(value, 8, 7)
    rest = value - high
    return jnp.concatenate([high, rest], axis=1).astype(jnp.bfloat16)


def packed_shares(projected, first, second):
    high = (first * FIRST_SCALE).astype(jnp.float16)
    high = lax.optimization_barrier(high)
    low = (first * FIRST_SCALE - high.astype(jnp.float32)) * LOW_SCALE
    rest = jnp.stack([low, projected * SHARE_SCALE, second * SECOND_SCALE])
    return jnp.concatenate([high[None], rest.astype(jnp.float16)])


def unpacked_shares(total):
    first = (total[0] + total[1] * (1.0 / LOW_SCALE)) * (1.0 / FIRST_SCALE)
    return total[2] * (1.0 / SHARE_SCALE), first, total[3] * (1.0 / SECOND_SCALE)


def on_device(partials, p_old, p_new, weight, m_old, v_old):
    core = lax.axis_index("core")
    z, yl = lax.axis_index("z"), lax.axis_index("yl")
    f32 = jnp.float32

    def sides(own, other, axis):
        return jnp.where(
            core == 0,
            jnp.concatenate([own, other], axis=axis),
            jnp.concatenate([other, own], axis=axis),
        )

    p_other = swap(p_new, "core", 1, 2)

    turn = [(a * 8 + b, a * 8 + (a ^ b)) for a in range(8) for b in range(8)]
    turned = lax.ppermute(jnp.stack([m_old, v_old]), ("z", "x", "yh"), turn)

    p_rank = lax.dynamic_index_in_dim(p_new.reshape(512, 8, 2, 64), yl, 2, keepdims=False)
    product = jnp.dot(p_rank.reshape(512, 512).T, p_old, preferred_element_type=f32)
    met = (lax.broadcasted_iota(jnp.int32, (512, 128), 0) // 64) ^ z
    margin = product[:, :128]
    for place in range(1, 8):
        margin = jnp.where(met == place, product[:, place * 128 : place * 128 + 128], margin)
    margin = margin + swap(margin, "core", 1, 2)
    margin = (margin * MARGIN_SCALE).astype(jnp.float16).reshape(8, 64, 128)

    grad = partials[0]
    theirs = cut(swap(grad, "core", 1, 2), core, 128, 1)
    ours = cut(grad, core, 128, 1)
    chip_sum = ((ours.astype(f32) + theirs.astype(f32)) * SCALE).astype(jnp.float16)
    sent = jnp.concatenate([chip_sum.reshape(8, 1024, 128), margin], axis=1)
    sent, turned = lax.optimization_barrier((sent, turned))
    rows = lax.all_to_all(sent, PAIRS, 0, 0, tiled=True)

    sums = lax.optimization_barrier(jnp.sum(rows.astype(f32), axis=0))
    grad_rows = sums[:1024] * (1.0 / SCALE)
    split = pieces(grad_rows)
    across = (((0,), (0,)), ((), ()))
    terms = lax.dot_general(
        p_new, cut(split, core, 512, 0), across, preferred_element_type=f32
    ) + lax.dot_general(
        p_other, cut(split, 1 - core, 512, 0), across, preferred_element_type=f32
    )
    projected = terms[:, :128] + terms[:, 128:]
    projected = (projected * PROJECTED_SCALE).astype(jnp.float16)
    projected, sums = lax.optimization_barrier((projected, sums))
    projected = lax.all_to_all(projected.reshape(16, 64, 128), PLANE, 0, 0, tiled=True)
    projected = jnp.sum(projected.astype(f32), axis=0) * (1.0 / PROJECTED_SCALE)
    moments_in = swap(cut(turned, 1 - core, 128, 2), "core", 1, 2)
    moments = sides(cut(turned, core, 128, 2), moments_in, 1)
    margin = sums[1024:] * (1.0 / MARGIN_SCALE)
    first = jnp.dot(margin, moments[0], precision=lax.Precision.HIGHEST)
    second = jnp.dot(margin * margin, moments[1], precision=lax.Precision.HIGHEST)
    shares = (projected, first, second)
    for bit in (2, 4, 1):
        packed = lax.optimization_barrier(packed_shares(*shares))
        ours, theirs = packed.astype(f32), swap(packed, "z", bit, 8).astype(f32)
        shares = unpacked_shares(ours + theirs)
    projected, first, second = shares

    m_new = beta_mean * first + (1.0 - beta_mean) * projected
    v_new = beta_square * second + (1.0 - beta_square) * projected * projected
    direction = (m_new / bias_mean / (jnp.sqrt(v_new / bias_square) + adam_epsilon)).astype(
        jnp.bfloat16
    )

    spread = jnp.broadcast_to(direction[None], (16, 64, 128))
    mine = lax.all_to_all(spread, PLANE, 0, 0, tiled=True).reshape(1024, 128)
    made = jnp.stack([m_new, v_new])
    near = swap(made, "yl", 1, 2)
    near, mine = lax.optimization_barrier((near, mine))
    other = swap(mine, "core", 1, 2)
    update = jnp.dot(p_new, sides(mine, other, 1), preferred_element_type=f32)
    update = with_layout_constraint(update, Layout((0, 1)))
    new_weight = weight - step_scale * update

    kept = jnp.where(core == yl, made, near)
    given = jnp.where(core == yl, near, made)
    made = sides(kept, swap(given, "core", 1, 2), 2)
    return (new_weight, made[0], made[1])


def solution(mesh):
    fine = Mesh(mesh.devices.reshape(SIZES), AXES)
    in_specs = (
        P(OUTER + DEV, None, None),
        P(DEV, None),
        P(DEV, None),
        P(DEV, None),
        P(DEV, None),
        P(DEV, None),
    )
    out_specs = (P(DEV, None), P(DEV, None), P(DEV, None))
    return jax.shard_map(
        on_device, mesh=fine, in_specs=in_specs, out_specs=out_specs, check_vma=False
    )
```
